256 devices in a mesh: rep: 32 (over z_hi, x, core), tp: 8 (over y, z_lo).
Axes of the slice: x: 4, y: 4, z: 8 (z_hi: 4, z_lo: 2; z = z_hi * 2 + z_lo), core: 2. Of those that a mesh axis runs over, the one named last changes fastest.
Arguments:
- queries: bfloat16 [64, 1024, 3072], P('rep', None, 'tp'), as said below
- keys: bfloat16 [64, 1024, 3072], P('rep', None, 'tp'), as said below
- values: bfloat16 [64, 1024, 3072], P('rep', None, 'tp'), may hold values from -6 to 6
- output_weight: bfloat16 [3072, 3072], P('tp'), may hold values from -0.109375 to 0.109375
- adapter_down_pool: bfloat16 [128, 3072, 64], P('rep', 'tp'), may hold values from -0.109375 to 0.109375
- adapter_up_pool: bfloat16 [128, 64, 3072], P('rep', None, 'tp'), may hold values from -0.3984375 to 0.3984375
- residual: bfloat16 [64, 1024, 3072], P('rep', None, 'tp'), may hold values from -3 to 3
- gate: bfloat16 [64, 3072], P('rep', 'tp'), may hold values from 0.5 to 1.5
- adapter_id: int32 [32], replicated, may hold values from 0 to 127
- adapter_slot: int32 [128], replicated, may hold values from 0 to 127, each once
- request_count: int32 [32], replicated, may hold values from 1 to 2, as said below
Outputs:
- updated: bfloat16 [64, 1024, 3072], P('rep', None, 'tp')
The draws below stay inside these ranges and needn't reach their ends.
Inputs may be any that keep to these rules, and one draw needn't show every extreme that they name: `request_count`: live slots of a replica; some replica has all 2 live, some has one. `adapter_slot`: slot s of the pool lies on replica index s // 4. `queries`: entries lie between -8 and 8. `keys`: entries lie between -8 and 8.
All inputs are finite; a program needn't handle non-finite values.
Results may differ from the reference program's by a relative error of at most 0.01.
Values may be sent and summed in bfloat16 or wider, within the bound.
No kernel may reach another device: no remote copies, remote signals or barrier semaphores. Data moves between devices by JAX's collectives and lax.ppermute only.
A program may use at most 128 MiB of HBM per device.

```python
import jax
import jax.numpy as jnp
from jax import lax

D = 3072
HEADS = 24
HD = 128
RANK = 64
SEQ = 1024
BATCH = 2
NADAPT = 128
N_REP = 32


def draw_keys(key, part):
    key = jax.random.fold_in(key, 1)
    shape = (N_REP * BATCH, SEQ, D)
    base = jnp.clip(1.5 * jax.random.normal(key, shape), -8.0, 8.0)
    return base.astype(jnp.bfloat16)


def draw_queries(key, part):
    key = jax.random.fold_in(key, 2)
    shape = (N_REP * BATCH, SEQ, D)
    base = jnp.clip(1.5 * jax.random.normal(key, shape), -8.0, 8.0)
    return base.astype(jnp.bfloat16)


def draw_request_count(key, part):
    key = jax.random.fold_in(key, 5)
    key_counts, key_full, key_single = jax.random.split(key, 3)
    counts = jax.random.randint(key_counts, (N_REP,), 1, BATCH + 1)
    full_at = jax.random.randint(key_full, (), 0, N_REP)
    single_at = (full_at + 1 + jax.random.randint(key_single, (), 0, N_REP - 1)) % N_REP
    indices = jnp.arange(N_REP, dtype=jnp.int32)
    counts = jnp.where(indices == full_at, BATCH, counts)
    counts = jnp.where(indices == single_at, 1, counts)
    return counts.astype(jnp.int32)


def touch_ends(array, own_key, least, high):
    longest = array.shape.index(max(array.shape))
    spots = []
    for shift in (0, 1):
        where = [jax.random.randint(jax.random.fold_in(own_key, axis), (), 0, length) for axis, length in enumerate(array.shape)]
        where[longest] = (where[longest] + shift) % array.shape[longest]
        spots.append(tuple(where))
    return array.at[spots[0]].set(least).at[spots[1]].set(high)


def shard_levels(stream_key, extent, cuts, low, largest):
    factor_of, own = 1.0, jax.random.fold_in(stream_key, 6)
    for axis_at, blocks in cuts:
        draws = jnp.exp(jax.random.uniform(jax.random.fold_in(own, axis_at), (blocks,), jnp.float32, low / len(cuts), largest / len(cuts)))
        factor_of = factor_of * jnp.repeat(draws, extent[axis_at] // blocks).reshape([-1 if axis == axis_at else 1 for axis in range(len(extent))])
    return factor_of


def scatter_about(rng, dims, spread, limit, cuts=(), kind=jnp.bfloat16):
    array = jax.random.normal(rng, dims, jnp.float32) * spread
    if len(cuts) > 0:
        array = shard_levels(rng, dims, cuts, -0.22, 0.18) * array
    return jnp.clip(array, min=-limit, max=limit).astype(kind)


def setup_inputs(seed: int = 0) -> dict:
    key_list = jax.random.split(jax.random.key(seed), 12)
    return {
        "queries": draw_queries(jax.random.fold_in(key_list[11], 71), 0),
        "keys": draw_keys(jax.random.fold_in(key_list[11], 71), 0),
        "values": scatter_about(key_list[2], (N_REP * BATCH, SEQ, D), 1.0, 6.0, ((0, 32), (2, 8))),
        "output_weight": scatter_about(key_list[3], (D, D), D ** -0.5, 0.109375, ((0, 8),)),
        "adapter_down_pool": scatter_about(key_list[4], (NADAPT, D, RANK), D ** -0.5, 0.109375, ((0, 32), (1, 8))),
        "adapter_up_pool": scatter_about(key_list[5], (NADAPT, RANK, D), 0.06, 0.3984375, ((0, 32), (2, 8))),
        "residual": scatter_about(key_list[6], (N_REP * BATCH, SEQ, D), 0.3, 3.0, ((0, 32), (2, 8))),
        "gate": jnp.clip(0.5 + 1.0 * jax.random.uniform(key_list[7], (N_REP * BATCH, D), jnp.float32) ** shard_levels(key_list[7], (N_REP * BATCH, D), ((0, 32), (1, 8)), -0.2, 0.2), 0.5, 1.5).astype(jnp.bfloat16),
        "adapter_id": touch_ends(jax.random.randint(key_list[8], (N_REP,), 0, NADAPT), jax.random.fold_in(key_list[8], 1), 0, NADAPT - 1).astype(jnp.int32),
        "adapter_slot": jax.random.permutation(key_list[9], NADAPT).astype(jnp.int32),
        "request_count": draw_request_count(jax.random.fold_in(key_list[11], 71), 0),
    }


def attend(query_rows, key_rows, value_rows):
    query_heads = query_rows.reshape(SEQ, HEADS, HD).astype(jnp.float32)
    key_heads = key_rows.reshape(SEQ, HEADS, HD).astype(jnp.float32)
    value_heads = value_rows.reshape(SEQ, HEADS, HD).astype(jnp.float32)
    score_scale = HD ** -0.5
    scores = jnp.einsum("qhd,khd->hqk", query_heads, key_heads) * score_scale
    highest = jnp.max(scores, axis=-1, keepdims=True)
    expos = jnp.exp(scores - highest)
    probs = (expos / jnp.sum(expos, axis=-1, keepdims=True)).astype(jnp.bfloat16)
    mixed = jnp.einsum("hqk,khd->qhd", probs.astype(jnp.float32), value_heads)
    return mixed.reshape(SEQ, D).astype(jnp.bfloat16)


def reference(queries, keys, values, output_weight, adapter_down_pool, adapter_up_pool, residual, gate, adapter_id, adapter_slot, request_count):
    query_all = queries.reshape(N_REP, BATCH, SEQ, D)
    key_all = keys.reshape(N_REP, BATCH, SEQ, D)
    value_all = values.reshape(N_REP, BATCH, SEQ, D)
    resid_all = residual.reshape(N_REP, BATCH, SEQ, D)
    gate_all = gate.reshape(N_REP, BATCH, D)

    def one_replica(replica):
        picked_adapter = adapter_slot[adapter_id[replica]]
        lowrank_adapter = jnp.dot(adapter_down_pool[picked_adapter], adapter_up_pool[picked_adapter], preferred_element_type=jnp.float32)
        merged_weight = (output_weight.astype(jnp.float32) + lowrank_adapter).astype(jnp.bfloat16)
        outputs = []
        for slot_number in range(BATCH):
            attended = attend(query_all[replica, slot_number], key_all[replica, slot_number], value_all[replica, slot_number])
            projected = jnp.dot(attended, merged_weight, preferred_element_type=jnp.float32)
            active = (slot_number < request_count[replica]).astype(jnp.float32)
            update = gate_all[replica, slot_number].astype(jnp.float32)[None, :] * projected * active
            outputs.append((resid_all[replica, slot_number].astype(jnp.float32) + update).astype(jnp.bfloat16))
        return jnp.stack(outputs)

    result = lax.map(one_replica, jnp.arange(N_REP, dtype=jnp.int32))
    return result.reshape(N_REP * BATCH, SEQ, D)
```

```python
import functools

import jax
import jax.numpy as jnp
from jax import lax
from jax.experimental import pallas as pl
from jax.experimental.pallas import tpu as pltpu
from jax.sharding import PartitionSpec as P

HD = 128
NY, NZ, NX, NC, NH = 4, 2, 4, 2, 4
LOG2E = 1.4426950408889634
VMEM = 60 * 1024 * 1024
TILE = 256
F32 = jnp.float32
BF16 = jnp.bfloat16


def table(move):
    pairs = []
    for h in range(NH):
        for x in range(NX):
            for c in range(NC):
                for y in range(NY):
                    for z in range(NZ):
                        here = ((h * NX + x) * NC + c) * NY * NZ + y * NZ + z
                        h2, x2, c2, y2, z2 = move(h, x, c, y, z)
                        h2, x2, c2, y2, z2 = h2 % NH, x2 % NX, c2 % NC, y2 % NY, z2 % NZ
                        there = ((h2 * NX + x2) * NC + c2) * NY * NZ + y2 * NZ + z2
                        pairs.append((here, there))
    return pairs


def send(array, move):
    return lax.ppermute(array, ("rep", "tp"), table(move))


def to_y(k):
    return lambda h, x, c, y, z: (h, x, c, y + k, z)


def to_x(k):
    return lambda h, x, c, y, z: (h, x + k, c, y, z)


def to_h(k):
    return lambda h, x, c, y, z: (h + k, x, c, y, z)


def swap_z(h, x, c, y, z):
    return (h, x, c, y, 1 - z)


def swap_core(h, x, c, y, z):
    return (h, x, 1 - c, y, z)


def other_z(h, x, c, y, z):
    return (h - 1 + 2 * z, x, c, y, 1 - z)


def params():
    return pltpu.CompilerParams(vmem_limit_bytes=VMEM)


def cost(flops, moved):
    return pl.CostEstimate(flops=flops, bytes_accessed=moved, transcendentals=0)


def attend_kernel(q_ref, k_ref, v_ref, out):
    rows = out.shape[0]
    k = k_ref[0]
    v = v_ref[0]
    v_one = jnp.concatenate([v, jnp.ones_like(v)], axis=1)
    factor = LOG2E * HD ** (-0.5)
    for begin in range(0, rows, TILE):
        part = slice(begin, begin + TILE)
        q = q_ref[0, part]
        s = lax.dot_general(q, k, (((1,), (1,)), ((), ())), preferred_element_type=F32)
        top = jnp.max(s, axis=1, keepdims=True)
        p = jnp.exp2((s - top) * factor).astype(BF16)
        o = jnp.dot(p, v_one, preferred_element_type=F32)
        out[part] = (o[:, :HD] / o[:, HD:]).astype(BF16)


def attend(queries, keys, values, chunk):
    b, first, rows = chunk
    seq, width = queries.shape[1:]
    whole = pl.BlockSpec((1, seq, HD), lambda h: (b, 0, h))
    return pl.pallas_call(
        attend_kernel,
        grid=(width // HD,),
        in_specs=[pl.BlockSpec((1, rows, HD), lambda h: (b, first // rows, h)), whole, whole],
        out_specs=pl.BlockSpec((rows, HD), lambda h: (0, h)),
        out_shape=jax.ShapeDtypeStruct((rows, width), BF16),
        compiler_params=params(),
        cost_estimate=cost(4 * rows * seq * width, 4 * (rows + seq) * width),
        name="attend",
    )(queries, keys, values)


def weight_specs(shift):
    def base(i, s):
        return (0, lax.rem(s[0] + shift, NY) * NZ + s[1])

    def swapped(i, s):
        return (0, lax.rem(s[0] + shift, NY))

    return base, swapped


def product(own, other, w_own, w_other):
    total = jnp.dot(own[...], w_own[...], preferred_element_type=F32)
    return total + jnp.dot(other[...], w_other[...], preferred_element_type=F32)


def far_kernel(marks, own, other, w_own, w_other, up_half, down_half):
    total = product(own, other, w_own, w_other).astype(BF16)
    half = up_half.shape[0]
    up_half[...] = total[:half]
    down_half[...] = total[half:]


def far(marks, own, other, weight, swapped):
    rows, width = own.shape
    base_map, swap_map = weight_specs(2)
    tile = pl.BlockSpec((rows, width), lambda i, s: (0, 0))
    half = pl.BlockSpec((rows // 2, width), lambda i, s: (0, 0))
    return pl.pallas_call(
        far_kernel,
        grid_spec=pltpu.PrefetchScalarGridSpec(
            num_scalar_prefetch=1,
            grid=(1,),
            in_specs=[
                tile,
                tile,
                pl.BlockSpec((width, width), base_map),
                pl.BlockSpec((width, width), swap_map),
            ],
            out_specs=[half, half],
        ),
        out_shape=[jax.ShapeDtypeStruct((rows // 2, width), BF16)] * 2,
        compiler_params=params(),
        cost_estimate=cost(4 * rows * width * width, 6 * rows * width),
        name="far",
    )(marks, own, other, weight, swapped)


def near_kernel(marks, own, other, w_own_r, w_other_r, w_own_l, w_other_l, got_r, got_l, out_r, out_l):
    half = got_r.shape[0]
    right = product(own, other, w_own_r, w_other_r)
    out_r[:half] = (right[:half] + got_r[...].astype(F32)).astype(BF16)
    out_r[half:] = right[half:].astype(BF16)
    left = product(own, other, w_own_l, w_other_l)
    out_l[:half] = left[:half].astype(BF16)
    out_l[half:] = (left[half:] + got_l[...].astype(F32)).astype(BF16)


def near(marks, own, other, weight, swapped, got_r, got_l):
    rows, width = own.shape
    tile = pl.BlockSpec((rows, width), lambda i, s: (0, 0))
    half = pl.BlockSpec((rows // 2, width), lambda i, s: (0, 0))
    specs = []
    for shift in (1, NY - 1):
        specs += [pl.BlockSpec((width, width), m) for m in weight_specs(shift)]
    return pl.pallas_call(
        near_kernel,
        grid_spec=pltpu.PrefetchScalarGridSpec(
            num_scalar_prefetch=1,
            grid=(1,),
            in_specs=[tile, tile] + specs + [half, half],
            out_specs=[tile, tile],
        ),
        out_shape=[jax.ShapeDtypeStruct((rows, width), BF16)] * 2,
        compiler_params=params(),
        cost_estimate=cost(8 * rows * width * width, 10 * rows * width),
        name="near",
    )(marks, own, other, weight, swapped, weight, swapped, got_r, got_l)


def lowrank_kernel(down_own, down_other, *refs):
    out = refs[-1]
    n = (len(refs) - 1) // 2
    dims = (((1,), (1,)), ((), ()))
    at = 0
    for own, other in zip(refs[:n], refs[n : 2 * n]):
        t = lax.dot_general(down_own[...], own[...], dims, preferred_element_type=F32)
        t = t + lax.dot_general(down_other[...], other[...], dims, preferred_element_type=F32)
        out[:, at : at + own.shape[0]] = t.astype(BF16)
        at += own.shape[0]


def lowrank(down_own, down_other, own, other):
    tokens = sum(a.shape[0] for a in own)
    width = own[0].shape[1]
    rank = down_own.shape[0]
    return pl.pallas_call(
        lowrank_kernel,
        out_shape=jax.ShapeDtypeStruct((rank, tokens), BF16),
        compiler_params=params(),
        cost_estimate=cost(4 * tokens * width * rank, 4 * tokens * width),
        name="lowrank",
    )(down_own, down_other, *own, *other)


def home_kernel(marks, own, other, w_own, w_other, got_r, got_l, t, up, residual, gate_ref, *rest):
    out = rest[-1]
    total = product(own, other, w_own, w_other)
    total = total + got_r[...].astype(F32) + got_l[...].astype(F32)
    dims = (((0,), (0,)), ((), ()))
    total = total + lax.dot_general(t[...], up[...], dims, preferred_element_type=F32)
    b = marks[3]
    live = (b < marks[2]).astype(F32)
    gate = gate_ref[...]
    g = jnp.where(b == 0, gate[0:1].astype(F32), gate[1:2].astype(F32)) * live
    out[0] = (residual[0].astype(F32) + g * total).astype(BF16)


def home(marks, chunk, own, other, weight, swapped, got_r, got_l, t, up, residual, gate, earlier):
    b, first, rows = chunk
    batch, seq, width = residual.shape
    base_map, swap_map = weight_specs(0)
    step = TILE
    tile = pl.BlockSpec((step, width), lambda i, s: (i, 0))
    place = pl.BlockSpec((1, step, width), lambda i, s: (b, first // step + i, 0))
    extra = [] if earlier is None else [earlier]
    return pl.pallas_call(
        home_kernel,
        grid_spec=pltpu.PrefetchScalarGridSpec(
            num_scalar_prefetch=1,
            grid=(rows // step,),
            in_specs=[
                tile,
                tile,
                pl.BlockSpec((width, width), base_map),
                pl.BlockSpec((width, width), swap_map),
                tile,
                tile,
                pl.BlockSpec((t.shape[0], step), lambda i, s: (0, (b * seq + first) // step + i)),
                pl.BlockSpec(up.shape, lambda i, s: (0, 0)),
                place,
                pl.BlockSpec((batch, width), lambda i, s: (0, 0)),
            ]
            + [pl.BlockSpec(memory_space=pl.ANY)] * len(extra),
            out_specs=place,
        ),
        out_shape=jax.ShapeDtypeStruct(residual.shape, BF16),
        input_output_aliases={11: 0} if extra else {},
        compiler_params=params(),
        cost_estimate=cost(4 * rows * width * width, 12 * rows * width),
        name="home",
    )(marks, own, other, weight, swapped, got_r, got_l, t, up, residual, gate, *extra)


def pick_adapter(down_pool, up_pool, wanted, rep, x, c, h):
    pool = jnp.stack([jnp.swapaxes(down_pool, 1, 2), up_pool], axis=1)
    slots = pool.shape[0]
    hits = wanted[:, None] == rep * slots + jnp.arange(slots, dtype=jnp.int32)
    hits = hits.reshape(NH, NX, NC, slots)

    def chosen(core):
        mask = lax.dynamic_index_in_dim(hits, core, 2, keepdims=False)
        total = None
        for n in range(slots):
            term = jnp.where(mask[:, :, n, None, None, None], pool[n], jnp.zeros((), BF16))
            total = term if total is None else total + term
        return total

    got = send(chosen(1 - c), swap_core)
    held = chosen(c) + got
    parts = [
        send(lax.dynamic_index_in_dim(held, lax.rem(x + d, NX), 1, keepdims=False), to_x(d))
        for d in range(1, NX)
    ]
    held = lax.dynamic_index_in_dim(held, x, 1, keepdims=False) + parts[0] + parts[1] + parts[2]
    parts = [
        send(lax.dynamic_index_in_dim(held, lax.rem(h + d, NH), 0, keepdims=False), to_h(d))
        for d in range(1, NH)
    ]
    own = lax.dynamic_index_in_dim(held, h, 0, keepdims=False) + parts[0] + parts[1] + parts[2]
    return own[0], own[1]


def per_device(
    queries,
    keys,
    values,
    output_weight,
    adapter_down_pool,
    adapter_up_pool,
    residual,
    gate,
    adapter_id,
    adapter_slot,
    request_count,
):
    rep = lax.axis_index("rep")
    tp = lax.axis_index("tp")
    c = lax.rem(rep, NC)
    x = lax.rem(lax.div(rep, NC), NX)
    h = lax.div(rep, NC * NX)
    y = lax.div(tp, NZ)
    z = lax.rem(tp, NZ)
    batch, seq, width = residual.shape

    pieces = [
        lax.dynamic_slice_in_dim(output_weight, (k * NZ + 1 - z) * width, width, 1) for k in range(NY)
    ]
    swapped = send(jnp.concatenate(pieces, axis=1), other_z)

    chunks = [(b, 0, seq) for b in range(batch)]
    own = [attend(queries, keys, values, chunk) for chunk in chunks]
    other = [send(a, swap_z) for a in own]

    wanted = adapter_slot[adapter_id]
    down, up = pick_adapter(adapter_down_pool, adapter_up_pool, wanted, rep, x, c, h)
    t = lowrank(down, send(down, swap_z), own, other)
    t = jnp.concatenate([t] + [send(t, to_y(k)) for k in range(1, NY)], axis=0)
    up = jnp.concatenate([up] * NY, axis=0)

    count = request_count[rep]
    result = None
    for chunk, mine, theirs in zip(chunks, own, other):
        marks = jnp.stack([y, z, count, jnp.int32(chunk[0])])
        up_half, down_half = far(marks, mine, theirs, output_weight, swapped)
        got_r = send(up_half, to_y(1))
        got_l = send(down_half, to_y(-1))
        right, left = near(marks, mine, theirs, output_weight, swapped, got_r, got_l)
        got_r = send(right, to_y(1))
        got_l = send(left, to_y(-1))
        result = home(
            marks, chunk, mine, theirs, output_weight, swapped, got_r, got_l, t, up, residual, gate, result
        )
    return result


def solution(mesh):
    placed = (
        P("rep", None, "tp"),
        P("rep", None, "tp"),
        P("rep", None, "tp"),
        P("tp", None),
        P("rep", "tp", None),
        P("rep", None, "tp"),
        P("rep", None, "tp"),
        P("rep", "tp"),
        P(),
        P(),
        P(),
    )
    return jax.shard_map(
        per_device, mesh=mesh, in_specs=placed, out_specs=P("rep", None, "tp"), check_vma=False
    )
```

```python
import functools

import jax
import jax.numpy as jnp
from jax import lax
from jax.experimental import pallas as pl
from jax.experimental.pallas import tpu as pltpu
from jax.sharding import PartitionSpec as P

HD = 128
NY, NZ, NX, NC, NH = 4, 2, 4, 2, 4
LOG2E = 1.4426950408889634
LARGE = 60 * 1024 * 1024
SMALL = 32 * 1024 * 1024
TILE = 256
STEP = 512
F32 = jnp.float32
BF16 = jnp.bfloat16


def table(move):
    pairs = []
    for h in range(NH):
        for x in range(NX):
            for c in range(NC):
                for y in range(NY):
                    for z in range(NZ):
                        here = ((h * NX + x) * NC + c) * NY * NZ + y * NZ + z
                        h2, x2, c2, y2, z2 = move(h, x, c, y, z)
                        h2, x2, c2, y2, z2 = h2 % NH, x2 % NX, c2 % NC, y2 % NY, z2 % NZ
                        there = ((h2 * NX + x2) * NC + c2) * NY * NZ + y2 * NZ + z2
                        pairs.append((here, there))
    return pairs


def send(array, move):
    return lax.ppermute(array, ("rep", "tp"), table(move))


def to_y(k):
    return lambda h, x, c, y, z: (h, x, c, y + k, z)


def to_x(k):
    return lambda h, x, c, y, z: (h, x + k, c, y, z)


def to_h(k):
    return lambda h, x, c, y, z: (h + k, x, c, y, z)


def swap_z(h, x, c, y, z):
    return (h, x, c, y, 1 - z)


def swap_core(h, x, c, y, z):
    return (h, x, 1 - c, y, z)


def pair_y(step):
    return lambda h, x, c, y, z: (h, x, c, y ^ step, z)


def pair_x(step):
    return lambda h, x, c, y, z: (h, x ^ step, c, y, z)


def other_z(h, x, c, y, z):
    return (h - 1 + 2 * z, x, c, y, 1 - z)


def params(size=SMALL):
    return pltpu.CompilerParams(vmem_limit_bytes=size)


def cost(flops, moved):
    return pl.CostEstimate(flops=flops, bytes_accessed=moved, transcendentals=0)


def attend_kernel(q_ref, k_ref, v_ref, out):
    rows = out.shape[0]
    k = k_ref[0]
    v = v_ref[0]
    v_one = jnp.concatenate([v, jnp.ones_like(v)], axis=1)
    factor = LOG2E * HD ** (-0.5)
    for begin in range(0, rows, TILE):
        part = slice(begin, begin + TILE)
        q = q_ref[0, part]
        s = lax.dot_general(q, k, (((1,), (1,)), ((), ())), preferred_element_type=F32)
        top = jnp.max(s, axis=1, keepdims=True)
        p = jnp.exp2((s - top) * factor).astype(BF16)
        o = jnp.dot(p, v_one, preferred_element_type=F32)
        out[part] = (o[:, :HD] / o[:, HD:]).astype(BF16)


def attend(queries, keys, values, chunk):
    b, first, rows = chunk
    seq, width = queries.shape[1:]
    whole = pl.BlockSpec((1, seq, HD), lambda h: (b, 0, h))
    return pl.pallas_call(
        attend_kernel,
        grid=(width // HD,),
        in_specs=[pl.BlockSpec((1, rows, HD), lambda h: (b, first // rows, h)), whole, whole],
        out_specs=pl.BlockSpec((rows, HD), lambda h: (0, h)),
        out_shape=jax.ShapeDtypeStruct((rows, width), BF16),
        compiler_params=params(LARGE),
        cost_estimate=cost(4 * rows * seq * width, 4 * (rows + seq) * width),
        name="attend",
    )(queries, keys, values)


def own_block(shift):
    return lambda i, s: (0, lax.rem(s[0] + shift, NY) * NZ + s[1])


def joined(first, second, axis):
    return jnp.concatenate([first[...], second[...]], axis=axis)


def after(value, *earlier):
    return lax.optimization_barrier((value, *earlier))[0]


def far_kernel(marks, own, other, w_own, w_other, *outs):
    w = joined(w_own, w_other, 0)
    total = jnp.dot(joined(own, other, 1), w, preferred_element_type=F32).astype(BF16)
    at = 0
    for out in outs:
        out[...] = total[at : at + out.shape[0]]
        at += out.shape[0]


def far(marks, own, other, weight, swapped, parts):
    rows, width = own.shape
    fixed = lambda i, s: (0, 0)
    tile = pl.BlockSpec((rows, width), fixed)
    return pl.pallas_call(
        far_kernel,
        grid_spec=pltpu.PrefetchScalarGridSpec(
            num_scalar_prefetch=1,
            grid=(1,),
            in_specs=[
                tile,
                tile,
                pl.BlockSpec((width, width), own_block(2)),
                pl.BlockSpec((width, width), fixed),
            ],
            out_specs=[pl.BlockSpec((rows // parts, width), fixed)] * parts,
        ),
        out_shape=[jax.ShapeDtypeStruct((rows // parts, width), BF16)] * parts,
        compiler_params=params(),
        cost_estimate=cost(4 * rows * width * width, 6 * rows * width),
        name="far",
    )(marks, own, other, weight, swapped)


def near_kernel(places, marks, own, other, w_r, w_l, r_other, l_other, *refs):
    outs = refs[-2:]
    width = w_r.shape[1]
    w = joined(w_r, w_l, 1)
    w = jnp.concatenate([w, joined(r_other, l_other, 1)], axis=0)
    total = jnp.dot(joined(own, other, 1), w, preferred_element_type=F32)
    for side, out in enumerate(outs):
        part = total[:, side * width : (side + 1) * width]
        out[...] = part.astype(BF16)
        for got, (where, first) in zip(refs, places):
            if where == side:
                last = first + got.shape[0]
                out[first:last] = (part[first:last] + got[...].astype(F32)).astype(BF16)


def near(marks, own, other, weight, first, gots, places):
    rows, width = own.shape
    fixed = lambda i, s: (0, 0)
    tile = pl.BlockSpec((rows, width), fixed)
    return pl.pallas_call(
        functools.partial(near_kernel, places),
        grid_spec=pltpu.PrefetchScalarGridSpec(
            num_scalar_prefetch=1,
            grid=(1,),
            in_specs=[
                tile,
                tile,
                pl.BlockSpec((width, width), own_block(1)),
                pl.BlockSpec((width, width), own_block(NY - 1)),
                pl.BlockSpec((width, width), lambda i, s: (0, 1)),
                pl.BlockSpec((width, width), lambda i, s: (0, 2)),
            ]
            + [pl.BlockSpec(got.shape, fixed) for got in gots],
            out_specs=[tile, tile],
        ),
        out_shape=[jax.ShapeDtypeStruct((rows, width), BF16)] * 2,
        compiler_params=params(),
        cost_estimate=cost(8 * rows * width * width, 10 * rows * width),
        name="near",
    )(marks, own, other, weight, weight, first, first, *gots)


def lowrank_kernel(down_own, down_other, *refs):
    out = refs[-1]
    n = (len(refs) - 1) // 2
    dims = (((1,), (1,)), ((), ()))
    at = 0
    for own, other in zip(refs[:n], refs[n : 2 * n]):
        t = lax.dot_general(down_own[...], own[...], dims, preferred_element_type=F32)
        t = t + lax.dot_general(down_other[...], other[...], dims, preferred_element_type=F32)
        out[:, at : at + own.shape[0]] = t.astype(BF16)
        at += own.shape[0]


def lowrank(down_own, down_other, own, other):
    tokens = sum(a.shape[0] for a in own)
    width = own[0].shape[1]
    rank = down_own.shape[0]
    return pl.pallas_call(
        lowrank_kernel,
        out_shape=jax.ShapeDtypeStruct((rank, tokens), BF16),
        compiler_params=params(),
        cost_estimate=cost(4 * tokens * width * rank, 4 * tokens * width),
        name="lowrank",
    )(down_own, down_other, *own, *other)


def home_kernel(b, n, marks, counts, own, other, w_own, w_other, t, up, residual, gate, *rest):
    out = rest[-1]
    w = joined(w_own, w_other, 0)
    total = jnp.dot(joined(own, other, 1), w, preferred_element_type=F32)
    for got in rest[:n]:
        total = total + got[...].astype(F32)
    dims = (((0,), (0,)), ((), ()))
    total = total + lax.dot_general(t[...], up[...], dims, preferred_element_type=F32)
    g = gate[...][b : b + 1].astype(F32) * (b < counts[marks[2]]).astype(F32)
    out[0] = (residual[0].astype(F32) + g * total).astype(BF16)


def home(marks, chunk, own, other, weight, swapped, gots, t, up, residual, gate, counts, earlier):
    b, first, rows = chunk
    batch, seq, width = residual.shape
    step = min(rows, STEP)
    fixed = lambda i, s, n: (0, 0)
    tile = pl.BlockSpec((step, width), lambda i, s, n: (i, 0))
    place = pl.BlockSpec((1, step, width), lambda i, s, n: (b, first // step + i, 0))
    extra = [] if earlier is None else [earlier]
    return pl.pallas_call(
        functools.partial(home_kernel, b, len(gots)),
        grid_spec=pltpu.PrefetchScalarGridSpec(
            num_scalar_prefetch=2,
            grid=(rows // step,),
            in_specs=[
                tile,
                tile,
                pl.BlockSpec((width, width), lambda i, s, n: (0, s[0] * NZ + s[1])),
                pl.BlockSpec((width, width), lambda i, s, n: (0, 3)),
                pl.BlockSpec((up.shape[0], step), lambda i, s, n: (0, (b * seq + first) // step + i)),
                pl.BlockSpec(up.shape, fixed),
                place,
                pl.BlockSpec((batch, width), fixed),
            ]
            + [tile] * len(gots)
            + [pl.BlockSpec(memory_space=pl.ANY)] * len(extra),
            out_specs=place,
        ),
        out_shape=jax.ShapeDtypeStruct(residual.shape, BF16),
        input_output_aliases={10 + len(gots): 0} if extra else {},
        compiler_params=params(),
        cost_estimate=cost(4 * rows * width * width, 12 * rows * width),
        name="home",
    )(marks, counts, own, other, weight, swapped, t, up, residual, gate, *gots, *extra)


def adapter_place(info, ids, slots, dest, count):
    return slots[ids[dest]] - info[2] * count


def choose_kernel(info, ids, slots, down, up, away):
    n = down.shape[0]
    for place in range(NH * NX):
        wanted = adapter_place(info, ids, slots, place * NC + 1 - info[3], n)
        away[place] = jnp.zeros(away.shape[1:], BF16)
        for k in range(n):

            @pl.when(wanted == k)
            def _():
                away[place, 0] = down[k]
                away[place, 1] = up[k]


def choose(info, ids, slots, down_pool, up_pool):
    rank, width = up_pool.shape[1:]
    smem = pl.BlockSpec(memory_space=pltpu.SMEM)
    vmem = pl.BlockSpec(memory_space=pltpu.VMEM)
    shape = (NH * NX, 2, rank, width)
    return pl.pallas_call(
        choose_kernel,
        in_specs=[smem] * 3 + [vmem] * 2,
        out_specs=vmem,
        out_shape=jax.ShapeDtypeStruct(shape, BF16),
        compiler_params=params(LARGE),
        cost_estimate=cost(0, 2 * NH * NX * 2 * rank * width),
        name="choose",
    )(info, ids, slots, down_pool, up_pool)


def keep_kernel(info, ids, slots, down, up, got, mine, away):
    n = down.shape[0]
    for h in range(NH):
        for i in range(NX // 2):
            for out, bit in ((mine, info[4]), (away, 1 - info[4])):
                place = h * NX + bit * (NX // 2) + i
                wanted = adapter_place(info, ids, slots, place * NC + info[3], n)
                out[h, i] = got[place]
                for k in range(n):

                    @pl.when(wanted == k)
                    def _():
                        out[h, i, 0] = got[place, 0] + down[k]
                        out[h, i, 1] = got[place, 1] + up[k]


def keep(info, ids, slots, down_pool, up_pool, got):
    rank, width = up_pool.shape[1:]
    smem = pl.BlockSpec(memory_space=pltpu.SMEM)
    vmem = pl.BlockSpec(memory_space=pltpu.VMEM)
    half = jax.ShapeDtypeStruct((NH, NX // 2, 2, rank, width), BF16)
    return pl.pallas_call(
        keep_kernel,
        in_specs=[smem] * 3 + [vmem] * 3,
        out_specs=[vmem] * 2,
        out_shape=[half, half],
        compiler_params=params(LARGE),
        cost_estimate=cost(0, 4 * NH * NX * 2 * rank * width),
        name="keep",
    )(info, ids, slots, down_pool, up_pool, got)


def merge_kernel(at, info, a, b, mine, away):
    bit = info[at]
    for p in range(a.shape[0]):
        for q in range(a.shape[2]):
            mine[p, q] = a[p, bit, q] + b[p, bit, q]
            away[p, q] = a[p, 1 - bit, q] + b[p, 1 - bit, q]


def merge(info, at, a, b, lead):
    whole = a.shape[-3:]
    count = a.size // (whole[0] * whole[1] * whole[2])
    split = (lead, 2, count // lead // 2) + whole
    half = jax.ShapeDtypeStruct((lead, count // lead // 2) + whole, BF16)
    vmem = pl.BlockSpec(memory_space=pltpu.VMEM)
    return pl.pallas_call(
        functools.partial(merge_kernel, at),
        in_specs=[pl.BlockSpec(memory_space=pltpu.SMEM), vmem, vmem],
        out_specs=[vmem, vmem],
        out_shape=[half, half],
        compiler_params=params(),
        cost_estimate=cost(0, 6 * a.size),
        name="merge",
    )(info, a.reshape(split), b.reshape(split))


def fan_kernel(info, a, b, *outs):
    for i, out in enumerate(outs):
        h = lax.rem(2 * info[6] + info[7] + i, NH)
        out[...] = a[h] + b[h]


def fan(info, a, b):
    shape = (NH,) + a.shape[-3:]
    vmem = pl.BlockSpec(memory_space=pltpu.VMEM)
    return pl.pallas_call(
        fan_kernel,
        in_specs=[pl.BlockSpec(memory_space=pltpu.SMEM), vmem, vmem],
        out_specs=[vmem] * NH,
        out_shape=[jax.ShapeDtypeStruct(shape[1:], BF16)] * NH,
        compiler_params=params(),
        cost_estimate=cost(0, 6 * a.size),
        name="fan",
    )(info, a.reshape(shape), b.reshape(shape))


def settle_kernel(a, b, c, d, down, up):
    for i, out in enumerate((down, up)):
        out[...] = a[i] + b[i] + c[i] + d[i]


def settle(parts):
    shape = parts[0].shape[1:]
    vmem = pl.BlockSpec(memory_space=pltpu.VMEM)
    return pl.pallas_call(
        settle_kernel,
        in_specs=[vmem] * NH,
        out_specs=[vmem] * 2,
        out_shape=[jax.ShapeDtypeStruct(shape, BF16)] * 2,
        compiler_params=params(),
        cost_estimate=cost(0, 10 * parts[0].size),
        name="settle",
    )(*parts)


def cut_kernel(info, a, b, c, d, out):
    width = a.shape[1]
    for i, block in enumerate((a, b, c, d)):
        out[:, i * width : (i + 1) * width] = block[...]


def cut(info, weight, width):
    def block(shift):
        return pl.BlockSpec((width, width), lambda i, s: (0, lax.rem(s[0] + shift, NY) * NZ + 1 - s[1]))

    return pl.pallas_call(
        cut_kernel,
        grid_spec=pltpu.PrefetchScalarGridSpec(
            num_scalar_prefetch=1,
            grid=(1,),
            in_specs=[block(shift) for shift in (2, 1, NY - 1, 0)],
            out_specs=pl.BlockSpec((width, NY * width), lambda i, s: (0, 0)),
        ),
        out_shape=jax.ShapeDtypeStruct((width, NY * width), BF16),
        compiler_params=params(LARGE),
        cost_estimate=cost(0, 16 * width * width),
        name="cut",
    )(info, *[weight] * 4)


def spread_kernel(marks, own, other, w_f, w_r, w_l, w_other, *outs):
    width = w_f.shape[1]
    w = jnp.concatenate([w_f[...], w_r[...], w_l[...]], axis=1)
    w = jnp.concatenate([w, w_other[...]], axis=0)
    total = jnp.dot(joined(own, other, 1), w, preferred_element_type=F32)
    for i, out in enumerate(outs):
        out[...] = total[:, i * width : (i + 1) * width].astype(BF16)


def spread(marks, own, other, weight, first):
    rows, width = own.shape
    fixed = lambda i, s: (0, 0)
    tile = pl.BlockSpec((rows, width), fixed)
    return pl.pallas_call(
        spread_kernel,
        grid_spec=pltpu.PrefetchScalarGridSpec(
            num_scalar_prefetch=1,
            grid=(1,),
            in_specs=[tile, tile]
            + [pl.BlockSpec((width, width), own_block(shift)) for shift in (2, 1, NY - 1)]
            + [pl.BlockSpec((width, 3 * width), fixed)],
            out_specs=[tile] * 3,
        ),
        out_shape=[jax.ShapeDtypeStruct((rows, width), BF16)] * 3,
        compiler_params=params(),
        cost_estimate=cost(12 * rows * width * width, 10 * rows * width),
        name="spread",
    )(marks, own, other, weight, weight, weight, first)


def per_device(
    queries,
    keys,
    values,
    output_weight,
    adapter_down_pool,
    adapter_up_pool,
    residual,
    gate,
    adapter_id,
    adapter_slot,
    request_count,
):
    rep = lax.axis_index("rep")
    tp = lax.axis_index("tp")
    c = lax.rem(rep, NC)
    x = lax.rem(lax.div(rep, NC), NX)
    h = lax.div(rep, NC * NX)
    y = lax.div(tp, NZ)
    z = lax.rem(tp, NZ)
    batch, seq, width = residual.shape

    info = jnp.stack([y, z, rep, c, lax.div(x, 2), lax.rem(x, 2), lax.div(h, 2), lax.rem(h, 2)])
    chunks = [(0, 0, seq // 2), (1, 0, seq), (0, seq // 2, seq // 2)]
    turns = (to_y(1), to_y(-1))
    own, other = [], []

    def mix(*earlier):
        a = attend(after(queries, *earlier), keys, values, chunks[len(own)])
        own.append(a)
        other.append(send(a, swap_z))

    def first_half(i, *earlier):
        return far(after(info, *earlier), own[i], other[i], output_weight, swapped, 2)

    def pass_on(i, halves):
        return [send(part, turn) for part, turn in zip(halves, turns)]

    def second_half(i, gots, *earlier):
        places = [(side, side * gots[0].shape[0]) for side in range(2)]
        marks = after(info, *earlier)
        sums = near(marks, own[i], other[i], output_weight, swapped, gots, places)
        return sums, [send(part, turn) for part, turn in zip(sums, turns)]

    piece = cut(info, output_weight, width)
    swapped = send(piece, other_z)
    pools = adapter_id, adapter_slot, jnp.swapaxes(adapter_down_pool, 1, 2), adapter_up_pool
    away = choose(after(info, piece), *pools)
    got = send(away, swap_core)
    mix(away)
    mix(own[0])
    held, away = keep(after(info, own[1], other[0]), *pools, got)
    got = send(away, pair_x(2))
    mix(away)
    messages = spread(after(info, own[2]), own[0], other[0], output_weight, swapped)
    home0 = [send(part, turn) for part, turn in zip(messages, (to_y(2),) + turns)]
    far1 = first_half(1, *messages)
    got1 = pass_on(1, far1)
    held, away = merge(after(info, *far1), 5, held, got, NH)
    got = send(away, pair_x(1))
    far2 = first_half(2, away)
    got2 = pass_on(2, far2)
    held = fan(after(info, *far2), held, got)
    parts = [held[0]] + [send(part, to_h(d + 1)) for d, part in enumerate(held[1:])]
    near1, home1 = second_half(1, got1, *held, *home0, *got2)
    near2, home2 = second_half(2, got2, *near1)
    parts[0] = after(parts[0], *near2)
    down, up = settle(parts)
    order = (0, 2, 1)
    t = lowrank(down, send(down, swap_z), [own[i] for i in order], [other[i] for i in order])
    t = after(t + send(t, pair_y(1)), *home1, *home2)
    t = t + send(t, pair_y(2))

    result = None
    for chunk, mine, theirs, gots in zip(chunks, own, other, (home0, home1, home2)):
        result = home(
            info, chunk, mine, theirs, output_weight, swapped, gots, t, up, residual, gate, request_count, result
        )
    return result


def solution(mesh):
    placed = (
        P("rep", None, "tp"),
        P("rep", None, "tp"),
        P("rep", None, "tp"),
        P("tp", None),
        P("rep", "tp", None),
        P("rep", None, "tp"),
        P("rep", None, "tp"),
        P("rep", "tp"),
        P(),
        P(),
        P(),
    )
    return jax.shard_map(
        per_device, mesh=mesh, in_specs=placed, out_specs=P("rep", None, "tp"), check_vma=False
    )
```

```python
import functools

import jax
import jax.numpy as jnp
from jax import lax
from jax.experimental import pallas as pl
from jax.experimental.pallas import tpu as pltpu
from jax.sharding import PartitionSpec as P

HD = 128
NY, NZ, NX, NC, NH = 4, 2, 4, 2, 4
LOG2E = 1.4426950408889634
LARGE = 60 * 1024 * 1024
SMALL = 32 * 1024 * 1024
TILE = 256
STEP = 512
F32 = jnp.float32
BF16 = jnp.bfloat16


def table(move):
    pairs = []
    for h in range(NH):
        for x in range(NX):
            for c in range(NC):
                for y in range(NY):
                    for z in range(NZ):
                        here = ((h * NX + x) * NC + c) * NY * NZ + y * NZ + z
                        h2, x2, c2, y2, z2 = move(h, x, c, y, z)
                        h2, x2, c2, y2, z2 = h2 % NH, x2 % NX, c2 % NC, y2 % NY, z2 % NZ
                        there = ((h2 * NX + x2) * NC + c2) * NY * NZ + y2 * NZ + z2
                        pairs.append((here, there))
    return pairs


def send(array, move):
    return lax.ppermute(array, ("rep", "tp"), table(move))


def to_y(k):
    return lambda h, x, c, y, z: (h, x, c, y + k, z)


def to_x(k):
    return lambda h, x, c, y, z: (h, x + k, c, y, z)


def to_h(k):
    return lambda h, x, c, y, z: (h + k, x, c, y, z)


def swap_z(h, x, c, y, z):
    return (h, x, c, y, 1 - z)


def swap_core(h, x, c, y, z):
    return (h, x, 1 - c, y, z)


def pair_y(step):
    return lambda h, x, c, y, z: (h, x, c, y ^ step, z)


def pair_x(step):
    return lambda h, x, c, y, z: (h, x ^ step, c, y, z)


def other_z(h, x, c, y, z):
    return (h - 1 + 2 * z, x, c, y, 1 - z)


def params(size=SMALL):
    return pltpu.CompilerParams(vmem_limit_bytes=size)


def cost(flops, moved):
    return pl.CostEstimate(flops=flops, bytes_accessed=moved, transcendentals=0)


def attend_kernel(q_ref, k_ref, v_ref, out):
    rows = out.shape[0]
    k = k_ref[0]
    v = v_ref[0]
    v_one = jnp.concatenate([v, jnp.ones_like(v)], axis=1)
    factor = LOG2E * HD ** (-0.5)
    for begin in range(0, rows, TILE):
        part = slice(begin, begin + TILE)
        q = q_ref[0, part]
        s = lax.dot_general(q, k, (((1,), (1,)), ((), ())), preferred_element_type=F32)
        top = jnp.max(s, axis=1, keepdims=True)
        p = jnp.exp2((s - top) * factor).astype(BF16)
        o = jnp.dot(p, v_one, preferred_element_type=F32)
        out[part] = (o[:, :HD] / o[:, HD:]).astype(BF16)


def attend(queries, keys, values, chunk):
    b, first, rows = chunk
    seq, width = queries.shape[1:]
    whole = pl.BlockSpec((1, seq, HD), lambda h: (b, 0, h))
    return pl.pallas_call(
        attend_kernel,
        grid=(width // HD,),
        in_specs=[pl.BlockSpec((1, rows, HD), lambda h: (b, first // rows, h)), whole, whole],
        out_specs=pl.BlockSpec((rows, HD), lambda h: (0, h)),
        out_shape=jax.ShapeDtypeStruct((rows, width), BF16),
        compiler_params=params(LARGE),
        cost_estimate=cost(4 * rows * seq * width, 4 * (rows + seq) * width),
        name="attend",
    )(queries, keys, values)


def own_block(shift):
    return lambda i, s: (0, lax.rem(s[0] + shift, NY) * NZ + s[1])


def joined(first, second, axis):
    return jnp.concatenate([first[...], second[...]], axis=axis)


def after(value, *earlier):
    return lax.optimization_barrier((value, *earlier))[0]


def far_kernel(marks, own, other, w_own, w_other, *outs):
    w = joined(w_own, w_other, 0)
    total = jnp.dot(joined(own, other, 1), w, preferred_element_type=F32).astype(BF16)
    at = 0
    for out in outs:
        out[...] = total[at : at + out.shape[0]]
        at += out.shape[0]


def far(marks, own, other, weight, swapped, parts):
    rows, width = own.shape
    fixed = lambda i, s: (0, 0)
    tile = pl.BlockSpec((rows, width), fixed)
    return pl.pallas_call(
        far_kernel,
        grid_spec=pltpu.PrefetchScalarGridSpec(
            num_scalar_prefetch=1,
            grid=(1,),
            in_specs=[
                tile,
                tile,
                pl.BlockSpec((width, width), own_block(2)),
                pl.BlockSpec((width, width), fixed),
            ],
            out_specs=[pl.BlockSpec((rows // parts, width), fixed)] * parts,
        ),
        out_shape=[jax.ShapeDtypeStruct((rows // parts, width), BF16)] * parts,
        compiler_params=params(),
        cost_estimate=cost(4 * rows * width * width, 6 * rows * width),
        name="far",
    )(marks, own, other, weight, swapped)


def near_kernel(places, marks, own, other, w_r, w_l, r_other, l_other, *refs):
    outs = refs[-2:]
    width = w_r.shape[1]
    w = joined(w_r, w_l, 1)
    w = jnp.concatenate([w, joined(r_other, l_other, 1)], axis=0)
    total = jnp.dot(joined(own, other, 1), w, preferred_element_type=F32)
    for side, out in enumerate(outs):
        part = total[:, side * width : (side + 1) * width]
        out[...] = part.astype(BF16)
        for got, (where, first) in zip(refs, places):
            if where == side:
                last = first + got.shape[0]
                out[first:last] = (part[first:last] + got[...].astype(F32)).astype(BF16)


def near(marks, own, other, weight, first, gots, places):
    rows, width = own.shape
    fixed = lambda i, s: (0, 0)
    tile = pl.BlockSpec((rows, width), fixed)
    return pl.pallas_call(
        functools.partial(near_kernel, places),
        grid_spec=pltpu.PrefetchScalarGridSpec(
            num_scalar_prefetch=1,
            grid=(1,),
            in_specs=[
                tile,
                tile,
                pl.BlockSpec((width, width), own_block(1)),
                pl.BlockSpec((width, width), own_block(NY - 1)),
                pl.BlockSpec((width, width), lambda i, s: (0, 1)),
                pl.BlockSpec((width, width), lambda i, s: (0, 2)),
            ]
            + [pl.BlockSpec(got.shape, fixed) for got in gots],
            out_specs=[tile, tile],
        ),
        out_shape=[jax.ShapeDtypeStruct((rows, width), BF16)] * 2,
        compiler_params=params(),
        cost_estimate=cost(8 * rows * width * width, 10 * rows * width),
        name="near",
    )(marks, own, other, weight, weight, first, first, *gots)


def lowrank_kernel(down_own, down_other, *refs):
    out = refs[-1]
    n = (len(refs) - 1) // 2
    dims = (((1,), (1,)), ((), ()))
    at = 0
    for own, other in zip(refs[:n], refs[n : 2 * n]):
        t = lax.dot_general(down_own[...], own[...], dims, preferred_element_type=F32)
        t = t + lax.dot_general(down_other[...], other[...], dims, preferred_element_type=F32)
        out[:, at : at + own.shape[0]] = t.astype(BF16)
        at += own.shape[0]


def lowrank(down_own, down_other, own, other):
    tokens = sum(a.shape[0] for a in own)
    width = own[0].shape[1]
    rank = down_own.shape[0]
    return pl.pallas_call(
        lowrank_kernel,
        out_shape=jax.ShapeDtypeStruct((rank, tokens), BF16),
        compiler_params=params(),
        cost_estimate=cost(4 * tokens * width * rank, 4 * tokens * width),
        name="lowrank",
    )(down_own, down_other, *own, *other)


def home_kernel(b, n, marks, counts, own, other, w_own, w_other, t, up, residual, gate, *rest):
    out = rest[-1]
    w = joined(w_own, w_other, 0)
    total = jnp.dot(joined(own, other, 1), w, preferred_element_type=F32)
    for got in rest[:n]:
        total = total + got[...].astype(F32)
    dims = (((0,), (0,)), ((), ()))
    total = total + lax.dot_general(t[...], up[...], dims, preferred_element_type=F32)
    g = gate[...][b : b + 1].astype(F32) * (b < counts[marks[2]]).astype(F32)
    out[0] = (residual[0].astype(F32) + g * total).astype(BF16)


def home(marks, chunk, own, other, weight, swapped, gots, t, up, residual, gate, counts, earlier):
    b, first, rows = chunk
    batch, seq, width = residual.shape
    step = min(rows, STEP)
    fixed = lambda i, s, n: (0, 0)
    tile = pl.BlockSpec((step, width), lambda i, s, n: (i, 0))
    place = pl.BlockSpec((1, step, width), lambda i, s, n: (b, first // step + i, 0))
    extra = [] if earlier is None else [earlier]
    return pl.pallas_call(
        functools.partial(home_kernel, b, len(gots)),
        grid_spec=pltpu.PrefetchScalarGridSpec(
            num_scalar_prefetch=2,
            grid=(rows // step,),
            in_specs=[
                tile,
                tile,
                pl.BlockSpec((width, width), lambda i, s, n: (0, s[0] * NZ + s[1])),
                pl.BlockSpec((width, width), lambda i, s, n: (0, 3)),
                pl.BlockSpec((up.shape[0], step), lambda i, s, n: (0, (b * seq + first) // step + i)),
                pl.BlockSpec(up.shape, fixed),
                place,
                pl.BlockSpec((batch, width), fixed),
            ]
            + [tile] * len(gots)
            + [pl.BlockSpec(memory_space=pl.ANY)] * len(extra),
            out_specs=place,
        ),
        out_shape=jax.ShapeDtypeStruct(residual.shape, BF16),
        input_output_aliases={10 + len(gots): 0} if extra else {},
        compiler_params=params(),
        cost_estimate=cost(4 * rows * width * width, 12 * rows * width),
        name="home",
    )(marks, counts, own, other, weight, swapped, t, up, residual, gate, *gots, *extra)


def adapter_place(info, ids, slots, dest, count):
    return slots[ids[dest]] - info[2] * count


def choose_kernel(info, ids, slots, down, up, away):
    n = down.shape[0]
    for place in range(NH * NX):
        wanted = adapter_place(info, ids, slots, place * NC + 1 - info[3], n)
        away[place] = jnp.zeros(away.shape[1:], BF16)
        for k in range(n):

            @pl.when(wanted == k)
            def _():
                away[place, 0] = down[k]
                away[place, 1] = up[k]


def choose(info, ids, slots, down_pool, up_pool):
    rank, width = up_pool.shape[1:]
    smem = pl.BlockSpec(memory_space=pltpu.SMEM)
    vmem = pl.BlockSpec(memory_space=pltpu.VMEM)
    shape = (NH * NX, 2, rank, width)
    return pl.pallas_call(
        choose_kernel,
        in_specs=[smem] * 3 + [vmem] * 2,
        out_specs=vmem,
        out_shape=jax.ShapeDtypeStruct(shape, BF16),
        compiler_params=params(LARGE),
        cost_estimate=cost(0, 2 * NH * NX * 2 * rank * width),
        name="choose",
    )(info, ids, slots, down_pool, up_pool)


def keep_kernel(info, ids, slots, down, up, got, mine, away):
    n = down.shape[0]
    for h in range(NH):
        for i in range(NX // 2):
            for out, bit in ((mine, info[4]), (away, 1 - info[4])):
                place = h * NX + bit * (NX // 2) + i
                wanted = adapter_place(info, ids, slots, place * NC + info[3], n)
                out[h, i] = got[place]
                for k in range(n):

                    @pl.when(wanted == k)
                    def _():
                        out[h, i, 0] = got[place, 0] + down[k]
                        out[h, i, 1] = got[place, 1] + up[k]


def keep(info, ids, slots, down_pool, up_pool, got):
    rank, width = up_pool.shape[1:]
    smem = pl.BlockSpec(memory_space=pltpu.SMEM)
    vmem = pl.BlockSpec(memory_space=pltpu.VMEM)
    half = jax.ShapeDtypeStruct((NH, NX // 2, 2, rank, width), BF16)
    return pl.pallas_call(
        keep_kernel,
        in_specs=[smem] * 3 + [vmem] * 3,
        out_specs=[vmem] * 2,
        out_shape=[half, half],
        compiler_params=params(LARGE),
        cost_estimate=cost(0, 4 * NH * NX * 2 * rank * width),
        name="keep",
    )(info, ids, slots, down_pool, up_pool, got)


def merge_kernel(at, info, a, b, mine, away):
    bit = info[at]
    for p in range(a.shape[0]):
        for q in range(a.shape[2]):
            mine[p, q] = a[p, bit, q] + b[p, bit, q]
            away[p, q] = a[p, 1 - bit, q] + b[p, 1 - bit, q]


def merge(info, at, a, b, lead):
    whole = a.shape[-3:]
    count = a.size // (whole[0] * whole[1] * whole[2])
    split = (lead, 2, count // lead // 2) + whole
    half = jax.ShapeDtypeStruct((lead, count // lead // 2) + whole, BF16)
    vmem = pl.BlockSpec(memory_space=pltpu.VMEM)
    return pl.pallas_call(
        functools.partial(merge_kernel, at),
        in_specs=[pl.BlockSpec(memory_space=pltpu.SMEM), vmem, vmem],
        out_specs=[vmem, vmem],
        out_shape=[half, half],
        compiler_params=params(),
        cost_estimate=cost(0, 6 * a.size),
        name="merge",
    )(info, a.reshape(split), b.reshape(split))


def fan_kernel(info, a, b, *outs):
    for i, out in enumerate(outs):
        h = lax.rem(2 * info[6] + info[7] + i, NH)
        out[...] = a[h] + b[h]


def fan(info, a, b):
    shape = (NH,) + a.shape[-3:]
    vmem = pl.BlockSpec(memory_space=pltpu.VMEM)
    return pl.pallas_call(
        fan_kernel,
        in_specs=[pl.BlockSpec(memory_space=pltpu.SMEM), vmem, vmem],
        out_specs=[vmem] * NH,
        out_shape=[jax.ShapeDtypeStruct(shape[1:], BF16)] * NH,
        compiler_params=params(),
        cost_estimate=cost(0, 6 * a.size),
        name="fan",
    )(info, a.reshape(shape), b.reshape(shape))


def settle_kernel(a, b, c, d, down, up):
    for i, out in enumerate((down, up)):
        out[...] = a[i] + b[i] + c[i] + d[i]


def settle(parts):
    shape = parts[0].shape[1:]
    vmem = pl.BlockSpec(memory_space=pltpu.VMEM)
    return pl.pallas_call(
        settle_kernel,
        in_specs=[vmem] * NH,
        out_specs=[vmem] * 2,
        out_shape=[jax.ShapeDtypeStruct(shape, BF16)] * 2,
        compiler_params=params(),
        cost_estimate=cost(0, 10 * parts[0].size),
        name="settle",
    )(*parts)


def cut_kernel(info, a, b, c, d, out):
    width = a.shape[1]
    for i, block in enumerate((a, b, c, d)):
        out[:, i * width : (i + 1) * width] = block[...]


def cut(info, weight, width):
    def block(shift):
        return pl.BlockSpec((width, width), lambda i, s: (0, lax.rem(s[0] + shift, NY) * NZ + 1 - s[1]))

    return pl.pallas_call(
        cut_kernel,
        grid_spec=pltpu.PrefetchScalarGridSpec(
            num_scalar_prefetch=1,
            grid=(1,),
            in_specs=[block(shift) for shift in (2, 1, NY - 1, 0)],
            out_specs=pl.BlockSpec((width, NY * width), lambda i, s: (0, 0)),
        ),
        out_shape=jax.ShapeDtypeStruct((width, NY * width), BF16),
        compiler_params=params(LARGE),
        cost_estimate=cost(0, 16 * width * width),
        name="cut",
    )(info, *[weight] * 4)


def spread_kernel(marks, own, other, w_f, w_r, w_l, w_other, *outs):
    width = w_f.shape[1]
    w = jnp.concatenate([w_f[...], w_r[...], w_l[...]], axis=1)
    w = jnp.concatenate([w, w_other[...]], axis=0)
    total = jnp.dot(joined(own, other, 1), w, preferred_element_type=F32)
    for i, out in enumerate(outs):
        out[...] = total[:, i * width : (i + 1) * width].astype(BF16)


def spread(marks, own, other, weight, first):
    rows, width = own.shape
    fixed = lambda i, s: (0, 0)
    tile = pl.BlockSpec((rows, width), fixed)
    return pl.pallas_call(
        spread_kernel,
        grid_spec=pltpu.PrefetchScalarGridSpec(
            num_scalar_prefetch=1,
            grid=(1,),
            in_specs=[tile, tile]
            + [pl.BlockSpec((width, width), own_block(shift)) for shift in (2, 1, NY - 1)]
            + [pl.BlockSpec((width, 3 * width), fixed)],
            out_specs=[tile] * 3,
        ),
        out_shape=[jax.ShapeDtypeStruct((rows, width), BF16)] * 3,
        compiler_params=params(),
        cost_estimate=cost(12 * rows * width * width, 10 * rows * width),
        name="spread",
    )(marks, own, other, weight, weight, weight, first)


def per_device(
    queries,
    keys,
    values,
    output_weight,
    adapter_down_pool,
    adapter_up_pool,
    residual,
    gate,
    adapter_id,
    adapter_slot,
    request_count,
):
    rep = lax.axis_index("rep")
    tp = lax.axis_index("tp")
    c = lax.rem(rep, NC)
    x = lax.rem(lax.div(rep, NC), NX)
    h = lax.div(rep, NC * NX)
    y = lax.div(tp, NZ)
    z = lax.rem(tp, NZ)
    batch, seq, width = residual.shape

    info = jnp.stack([y, z, rep, c, lax.div(x, 2), lax.rem(x, 2), lax.div(h, 2), lax.rem(h, 2)])
    chunks = [(0, 0, seq // 2), (1, 0, seq), (0, seq // 2, seq // 2)]
    turns = (to_y(1), to_y(-1))
    own, other = [], []

    def mix(*earlier):
        a = attend(after(queries, *earlier), keys, values, chunks[len(own)])
        own.append(a)
        other.append(send(a, swap_z))

    def first_half(i, *earlier):
        return far(after(info, *earlier), own[i], other[i], output_weight, swapped, 2)

    def pass_on(i, halves):
        return [send(part, turn) for part, turn in zip(halves, turns)]

    def second_half(i, gots, *earlier):
        places = [(side, side * gots[0].shape[0]) for side in range(2)]
        marks = after(info, *earlier)
        sums = near(marks, own[i], other[i], output_weight, swapped, gots, places)
        return sums, [send(part, turn) for part, turn in zip(sums, turns)]

    piece = cut(info, output_weight, width)
    swapped = send(piece, other_z)
    pools = adapter_id, adapter_slot, jnp.swapaxes(adapter_down_pool, 1, 2), adapter_up_pool
    away = choose(after(info, piece), *pools)
    got = send(away, swap_core)
    mix(away)
    mix(own[0])
    held, away = keep(after(info, own[1], other[0]), *pools, got)
    got = send(away, pair_x(2))
    mix(away)
    messages = spread(after(info, own[2]), own[0], other[0], output_weight, swapped)
    home0 = [send(part, turn) for part, turn in zip(messages, (to_y(2),) + turns)]
    far1 = first_half(1, *messages)
    got1 = pass_on(1, far1)
    held, away = merge(after(info, *far1), 5, held, got, NH)
    got = send(away, pair_x(1))
    far2 = first_half(2, away)
    got2 = pass_on(2, far2)
    held = fan(after(info, *far2), held, got)
    parts = [held[0]] + [send(part, to_h(d + 1)) for d, part in enumerate(held[1:])]
    near1, home1 = second_half(1, got1, *held, *home0, *got2)
    near2, home2 = second_half(2, got2, *near1)
    parts[0] = after(parts[0], *near2)
    down, up = settle(parts)
    order = (0, 2, 1)
    t = lowrank(down, send(down, swap_z), [own[i] for i in order], [other[i] for i in order])
    late = after(t, *home1, *home2)
    t = t + send(t, to_y(1)) + send(t, to_y(-1)) + send(late, to_y(2))

    result = None
    for chunk, mine, theirs, gots in zip(chunks, own, other, (home0, home1, home2)):
        result = home(
            info, chunk, mine, theirs, output_weight, swapped, gots, t, up, residual, gate, request_count, result
        )
    return result


def solution(mesh):
    placed = (
        P("rep", None, "tp"),
        P("rep", None, "tp"),
        P("rep", None, "tp"),
        P("tp", None),
        P("rep", "tp", None),
        P("rep", None, "tp"),
        P("rep", None, "tp"),
        P("rep", "tp"),
        P(),
        P(),
        P(),
    )
    return jax.shard_map(
        per_device, mesh=mesh, in_specs=placed, out_specs=P("rep", None, "tp"), check_vma=False
    )
```

```python
import functools

import jax
import jax.numpy as jnp
from jax import lax
from jax.experimental import pallas as pl
from jax.experimental.pallas import tpu as pltpu
from jax.sharding import PartitionSpec as P

HD = 128
NY, NZ, NX, NC, NH = 4, 2, 4, 2, 4
LOG2E = 1.4426950408889634
LARGE = 60 * 1024 * 1024
SMALL = 32 * 1024 * 1024
TILE = 256
STEP = 512
F32 = jnp.float32
BF16 = jnp.bfloat16


def table(move):
    pairs = []
    for h in range(NH):
        for x in range(NX):
            for c in range(NC):
                for y in range(NY):
                    for z in range(NZ):
                        here = ((h * NX + x) * NC + c) * NY * NZ + y * NZ + z
                        h2, x2, c2, y2, z2 = move(h, x, c, y, z)
                        h2, x2, c2, y2, z2 = h2 % NH, x2 % NX, c2 % NC, y2 % NY, z2 % NZ
                        there = ((h2 * NX + x2) * NC + c2) * NY * NZ + y2 * NZ + z2
                        pairs.append((here, there))
    return pairs


def send(array, move):
    return lax.ppermute(array, ("rep", "tp"), table(move))


def to_y(k):
    return lambda h, x, c, y, z: (h, x, c, y + k, z)


def to_x(k):
    return lambda h, x, c, y, z: (h, x + k, c, y, z)


def to_h(k):
    return lambda h, x, c, y, z: (h + k, x, c, y, z)


def swap_z(h, x, c, y, z):
    return (h, x, c, y, 1 - z)


def swap_core(h, x, c, y, z):
    return (h, x, 1 - c, y, z)


def pair_y(step):
    return lambda h, x, c, y, z: (h, x, c, y ^ step, z)


def pair_x(step):
    return lambda h, x, c, y, z: (h, x ^ step, c, y, z)


def other_z(h, x, c, y, z):
    return (h - 1 + 2 * z, x, c, y, 1 - z)


def params(size=SMALL):
    return pltpu.CompilerParams(vmem_limit_bytes=size)


def cost(flops, moved):
    return pl.CostEstimate(flops=flops, bytes_accessed=moved, transcendentals=0)


def attend_kernel(q_ref, k_ref, v_ref, out):
    rows = out.shape[0]
    k = k_ref[0]
    v = v_ref[0]
    v_one = jnp.concatenate([v, jnp.ones_like(v)], axis=1)
    factor = LOG2E * HD ** (-0.5)
    for begin in range(0, rows, TILE):
        part = slice(begin, begin + TILE)
        q = q_ref[0, part]
        s = lax.dot_general(q, k, (((1,), (1,)), ((), ())), preferred_element_type=F32)
        top = jnp.max(s, axis=1, keepdims=True)
        p = jnp.exp2((s - top) * factor).astype(BF16)
        o = jnp.dot(p, v_one, preferred_element_type=F32)
        out[part] = (o[:, :HD] / o[:, HD:]).astype(BF16)


def attend(queries, keys, values, chunk):
    b, first, rows = chunk
    seq, width = queries.shape[1:]
    whole = pl.BlockSpec((1, seq, HD), lambda h: (b, 0, h))
    return pl.pallas_call(
        attend_kernel,
        grid=(width // HD,),
        in_specs=[pl.BlockSpec((1, rows, HD), lambda h: (b, first // rows, h)), whole, whole],
        out_specs=pl.BlockSpec((rows, HD), lambda h: (0, h)),
        out_shape=jax.ShapeDtypeStruct((rows, width), BF16),
        compiler_params=params(LARGE),
        cost_estimate=cost(4 * rows * seq * width, 4 * (rows + seq) * width),
        name="attend",
    )(queries, keys, values)


def own_block(shift):
    return lambda i, s: (0, lax.rem(s[0] + shift, NY) * NZ + s[1])


def joined(first, second, axis):
    return jnp.concatenate([first[...], second[...]], axis=axis)


def after(value, *earlier):
    return lax.optimization_barrier((value, *earlier))[0]


def far_kernel(marks, own, other, w_own, w_other, *outs):
    w = joined(w_own, w_other, 0)
    total = jnp.dot(joined(own, other, 1), w, preferred_element_type=F32).astype(BF16)
    at = 0
    for out in outs:
        out[...] = total[at : at + out.shape[0]]
        at += out.shape[0]


def far(marks, own, other, weight, swapped, parts):
    rows, width = own.shape
    fixed = lambda i, s: (0, 0)
    tile = pl.BlockSpec((rows, width), fixed)
    return pl.pallas_call(
        far_kernel,
        grid_spec=pltpu.PrefetchScalarGridSpec(
            num_scalar_prefetch=1,
            grid=(1,),
            in_specs=[
                tile,
                tile,
                pl.BlockSpec((width, width), own_block(2)),
                pl.BlockSpec((width, width), fixed),
            ],
            out_specs=[pl.BlockSpec((rows // parts, width), fixed)] * parts,
        ),
        out_shape=[jax.ShapeDtypeStruct((rows // parts, width), BF16)] * parts,
        compiler_params=params(),
        cost_estimate=cost(4 * rows * width * width, 6 * rows * width),
        name="far",
    )(marks, own, other, weight, swapped)


def near_kernel(places, marks, own, other, w_r, w_l, r_other, l_other, *refs):
    outs = refs[-2:]
    width = w_r.shape[1]
    w = joined(w_r, w_l, 1)
    w = jnp.concatenate([w, joined(r_other, l_other, 1)], axis=0)
    total = jnp.dot(joined(own, other, 1), w, preferred_element_type=F32)
    for side, out in enumerate(outs):
        part = total[:, side * width : (side + 1) * width]
        out[...] = part.astype(BF16)
        for got, (where, first) in zip(refs, places):
            if where == side:
                last = first + got.shape[0]
                out[first:last] = (part[first:last] + got[...].astype(F32)).astype(BF16)


def near(marks, own, other, weight, first, gots, places):
    rows, width = own.shape
    fixed = lambda i, s: (0, 0)
    tile = pl.BlockSpec((rows, width), fixed)
    return pl.pallas_call(
        functools.partial(near_kernel, places),
        grid_spec=pltpu.PrefetchScalarGridSpec(
            num_scalar_prefetch=1,
            grid=(1,),
            in_specs=[
                tile,
                tile,
                pl.BlockSpec((width, width), own_block(1)),
                pl.BlockSpec((width, width), own_block(NY - 1)),
                pl.BlockSpec((width, width), lambda i, s: (0, 1)),
                pl.BlockSpec((width, width), lambda i, s: (0, 2)),
            ]
            + [pl.BlockSpec(got.shape, fixed) for got in gots],
            out_specs=[tile, tile],
        ),
        out_shape=[jax.ShapeDtypeStruct((rows, width), BF16)] * 2,
        compiler_params=params(),
        cost_estimate=cost(8 * rows * width * width, 10 * rows * width),
        name="near",
    )(marks, own, other, weight, weight, first, first, *gots)


def lowrank_kernel(down_own, down_other, *refs):
    out = refs[-1]
    n = (len(refs) - 1) // 2
    dims = (((1,), (1,)), ((), ()))
    at = 0
    for own, other in zip(refs[:n], refs[n : 2 * n]):
        t = lax.dot_general(down_own[...], own[...], dims, preferred_element_type=F32)
        t = t + lax.dot_general(down_other[...], other[...], dims, preferred_element_type=F32)
        out[:, at : at + own.shape[0]] = t.astype(BF16)
        at += own.shape[0]


def lowrank(down_own, down_other, own, other):
    tokens = sum(a.shape[0] for a in own)
    width = own[0].shape[1]
    rank = down_own.shape[0]
    return pl.pallas_call(
        lowrank_kernel,
        out_shape=jax.ShapeDtypeStruct((rank, tokens), BF16),
        compiler_params=params(),
        cost_estimate=cost(4 * tokens * width * rank, 4 * tokens * width),
        name="lowrank",
    )(down_own, down_other, *own, *other)


def home_kernel(b, n, marks, counts, own, other, w_own, w_other, t, up, residual, gate, *rest):
    out = rest[-1]
    w = joined(w_own, w_other, 0)
    total = jnp.dot(joined(own, other, 1), w, preferred_element_type=F32)
    for got in rest[:n]:
        total = total + got[...].astype(F32)
    dims = (((0,), (0,)), ((), ()))
    total = total + lax.dot_general(t[...], up[...], dims, preferred_element_type=F32)
    g = gate[...][b : b + 1].astype(F32) * (b < counts[marks[2]]).astype(F32)
    out[0] = (residual[0].astype(F32) + g * total).astype(BF16)


def home(marks, chunk, own, other, weight, swapped, gots, t, up, residual, gate, counts, earlier):
    b, first, rows = chunk
    batch, seq, width = residual.shape
    step = min(rows, STEP)
    fixed = lambda i, s, n: (0, 0)
    tile = pl.BlockSpec((step, width), lambda i, s, n: (i, 0))
    place = pl.BlockSpec((1, step, width), lambda i, s, n: (b, first // step + i, 0))
    extra = [] if earlier is None else [earlier]
    return pl.pallas_call(
        functools.partial(home_kernel, b, len(gots)),
        grid_spec=pltpu.PrefetchScalarGridSpec(
            num_scalar_prefetch=2,
            grid=(rows // step,),
            in_specs=[
                tile,
                tile,
                pl.BlockSpec((width, width), lambda i, s, n: (0, s[0] * NZ + s[1])),
                pl.BlockSpec((width, width), lambda i, s, n: (0, 3)),
                pl.BlockSpec((up.shape[0], step), lambda i, s, n: (0, (b * seq + first) // step + i)),
                pl.BlockSpec(up.shape, fixed),
                place,
                pl.BlockSpec((batch, width), fixed),
            ]
            + [tile] * len(gots)
            + [pl.BlockSpec(memory_space=pl.ANY)] * len(extra),
            out_specs=place,
        ),
        out_shape=jax.ShapeDtypeStruct(residual.shape, BF16),
        input_output_aliases={10 + len(gots): 0} if extra else {},
        compiler_params=params(),
        cost_estimate=cost(4 * rows * width * width, 12 * rows * width),
        name="home",
    )(marks, counts, own, other, weight, swapped, t, up, residual, gate, *gots, *extra)


def adapter_place(info, ids, slots, dest, count):
    return slots[ids[dest]] - info[2] * count


def choose_kernel(info, ids, slots, down, up, away):
    n = down.shape[0]
    for place in range(NH * NX):
        wanted = adapter_place(info, ids, slots, place * NC + 1 - info[3], n)
        away[place] = jnp.zeros(away.shape[1:], BF16)
        for k in range(n):

            @pl.when(wanted == k)
            def _():
                away[place, 0] = down[k]
                away[place, 1] = up[k]


def choose(info, ids, slots, down_pool, up_pool):
    rank, width = up_pool.shape[1:]
    smem = pl.BlockSpec(memory_space=pltpu.SMEM)
    vmem = pl.BlockSpec(memory_space=pltpu.VMEM)
    shape = (NH * NX, 2, rank, width)
    return pl.pallas_call(
        choose_kernel,
        in_specs=[smem] * 3 + [vmem] * 2,
        out_specs=vmem,
        out_shape=jax.ShapeDtypeStruct(shape, BF16),
        compiler_params=params(LARGE),
        cost_estimate=cost(0, 2 * NH * NX * 2 * rank * width),
        name="choose",
    )(info, ids, slots, down_pool, up_pool)


def keep_kernel(info, ids, slots, down, up, got, mine, away):
    n = down.shape[0]
    for h in range(NH):
        for i in range(NX // 2):
            for out, bit in ((mine, info[4]), (away, 1 - info[4])):
                place = h * NX + bit * (NX // 2) + i
                wanted = adapter_place(info, ids, slots, place * NC + info[3], n)
                out[h, i] = got[place]
                for k in range(n):

                    @pl.when(wanted == k)
                    def _():
                        out[h, i, 0] = got[place, 0] + down[k]
                        out[h, i, 1] = got[place, 1] + up[k]


def keep(info, ids, slots, down_pool, up_pool, got):
    rank, width = up_pool.shape[1:]
    smem = pl.BlockSpec(memory_space=pltpu.SMEM)
    vmem = pl.BlockSpec(memory_space=pltpu.VMEM)
    half = jax.ShapeDtypeStruct((NH, NX // 2, 2, rank, width), BF16)
    return pl.pallas_call(
        keep_kernel,
        in_specs=[smem] * 3 + [vmem] * 3,
        out_specs=[vmem] * 2,
        out_shape=[half, half],
        compiler_params=params(LARGE),
        cost_estimate=cost(0, 4 * NH * NX * 2 * rank * width),
        name="keep",
    )(info, ids, slots, down_pool, up_pool, got)


def merge_kernel(at, info, a, b, mine, away):
    bit = info[at]
    for p in range(a.shape[0]):
        for q in range(a.shape[2]):
            mine[p, q] = a[p, bit, q] + b[p, bit, q]
            away[p, q] = a[p, 1 - bit, q] + b[p, 1 - bit, q]


def merge(info, at, a, b, lead):
    whole = a.shape[-3:]
    count = a.size // (whole[0] * whole[1] * whole[2])
    split = (lead, 2, count // lead // 2) + whole
    half = jax.ShapeDtypeStruct((lead, count // lead // 2) + whole, BF16)
    vmem = pl.BlockSpec(memory_space=pltpu.VMEM)
    return pl.pallas_call(
        functools.partial(merge_kernel, at),
        in_specs=[pl.BlockSpec(memory_space=pltpu.SMEM), vmem, vmem],
        out_specs=[vmem, vmem],
        out_shape=[half, half],
        compiler_params=params(),
        cost_estimate=cost(0, 6 * a.size),
        name="merge",
    )(info, a.reshape(split), b.reshape(split))


def fan_kernel(info, a, b, *outs):
    for i, out in enumerate(outs):
        h = lax.rem(2 * info[6] + info[7] + i, NH)
        out[...] = a[h] + b[h]


def fan(info, a, b):
    shape = (NH,) + a.shape[-3:]
    vmem = pl.BlockSpec(memory_space=pltpu.VMEM)
    return pl.pallas_call(
        fan_kernel,
        in_specs=[pl.BlockSpec(memory_space=pltpu.SMEM), vmem, vmem],
        out_specs=[vmem] * NH,
        out_shape=[jax.ShapeDtypeStruct(shape[1:], BF16)] * NH,
        compiler_params=params(),
        cost_estimate=cost(0, 6 * a.size),
        name="fan",
    )(info, a.reshape(shape), b.reshape(shape))


def settle_kernel(a, b, c, d, down, up):
    for i, out in enumerate((down, up)):
        out[...] = a[i] + b[i] + c[i] + d[i]


def settle(parts):
    shape = parts[0].shape[1:]
    vmem = pl.BlockSpec(memory_space=pltpu.VMEM)
    return pl.pallas_call(
        settle_kernel,
        in_specs=[vmem] * NH,
        out_specs=[vmem] * 2,
        out_shape=[jax.ShapeDtypeStruct(shape, BF16)] * 2,
        compiler_params=params(),
        cost_estimate=cost(0, 10 * parts[0].size),
        name="settle",
    )(*parts)


def cut_kernel(info, a, b, c, d, out):
    width = a.shape[1]
    for i, block in enumerate((a, b, c, d)):
        out[:, i * width : (i + 1) * width] = block[...]


def cut(info, weight, width):
    def block(shift):
        return pl.BlockSpec((width, width), lambda i, s: (0, lax.rem(s[0] + shift, NY) * NZ + 1 - s[1]))

    return pl.pallas_call(
        cut_kernel,
        grid_spec=pltpu.PrefetchScalarGridSpec(
            num_scalar_prefetch=1,
            grid=(1,),
            in_specs=[block(shift) for shift in (2, 1, NY - 1, 0)],
            out_specs=pl.BlockSpec((width, NY * width), lambda i, s: (0, 0)),
        ),
        out_shape=jax.ShapeDtypeStruct((width, NY * width), BF16),
        compiler_params=params(LARGE),
        cost_estimate=cost(0, 16 * width * width),
        name="cut",
    )(info, *[weight] * 4)


def spread_kernel(marks, own, other, w_f, w_r, w_l, w_other, *outs):
    width = w_f.shape[1]
    w = jnp.concatenate([w_f[...], w_r[...], w_l[...]], axis=1)
    w = jnp.concatenate([w, w_other[...]], axis=0)
    total = jnp.dot(joined(own, other, 1), w, preferred_element_type=F32)
    for i, out in enumerate(outs):
        out[...] = total[:, i * width : (i + 1) * width].astype(BF16)


def spread(marks, own, other, weight, first):
    rows, width = own.shape
    fixed = lambda i, s: (0, 0)
    tile = pl.BlockSpec((rows, width), fixed)
    return pl.pallas_call(
        spread_kernel,
        grid_spec=pltpu.PrefetchScalarGridSpec(
            num_scalar_prefetch=1,
            grid=(1,),
            in_specs=[tile, tile]
            + [pl.BlockSpec((width, width), own_block(shift)) for shift in (2, 1, NY - 1)]
            + [pl.BlockSpec((width, 3 * width), fixed)],
            out_specs=[tile] * 3,
        ),
        out_shape=[jax.ShapeDtypeStruct((rows, width), BF16)] * 3,
        compiler_params=params(),
        cost_estimate=cost(12 * rows * width * width, 10 * rows * width),
        name="spread",
    )(marks, own, other, weight, weight, weight, first)


def per_device(
    queries,
    keys,
    values,
    output_weight,
    adapter_down_pool,
    adapter_up_pool,
    residual,
    gate,
    adapter_id,
    adapter_slot,
    request_count,
):
    rep = lax.axis_index("rep")
    tp = lax.axis_index("tp")
    c = lax.rem(rep, NC)
    x = lax.rem(lax.div(rep, NC), NX)
    h = lax.div(rep, NC * NX)
    y = lax.div(tp, NZ)
    z = lax.rem(tp, NZ)
    batch, seq, width = residual.shape

    info = jnp.stack([y, z, rep, c, lax.div(x, 2), lax.rem(x, 2), lax.div(h, 2), lax.rem(h, 2)])
    chunks = [(0, 0, seq // 2), (1, 0, seq), (0, seq // 2, seq // 2)]
    turns = (to_y(1), to_y(-1))
    own, other = [], []

    def mix(*earlier):
        a = attend(after(queries, *earlier), keys, values, chunks[len(own)])
        own.append(a)
        other.append(send(a, swap_z))

    def first_half(i, *earlier):
        return far(after(info, *earlier), own[i], other[i], output_weight, swapped, 2)

    def pass_on(i, halves):
        return [send(part, turn) for part, turn in zip(halves, turns)]

    def second_half(i, gots, *earlier):
        places = [(side, side * gots[0].shape[0]) for side in range(2)]
        marks = after(info, *earlier)
        sums = near(marks, own[i], other[i], output_weight, swapped, gots, places)
        return sums, [send(part, turn) for part, turn in zip(sums, turns)]

    piece = cut(info, output_weight, width)
    swapped = send(piece, other_z)
    pools = adapter_id, adapter_slot, jnp.swapaxes(adapter_down_pool, 1, 2), adapter_up_pool
    away = choose(after(info, piece), *pools)
    got = send(away, swap_core)
    mix(away)
    mix(own[0])
    held, away = keep(after(info, own[1], other[0]), *pools, got)
    got = send(away, pair_x(2))
    mix(away)
    messages = spread(after(info, own[2]), own[0], other[0], output_weight, swapped)
    home0 = [send(part, turn) for part, turn in zip(messages, (to_y(2),) + turns)]
    far1 = first_half(1, *messages)
    got1 = pass_on(1, far1)
    held, away = merge(after(info, *far1), 5, held, got, NH)
    got = send(away, pair_x(1))
    last = spread(after(info, away), own[2], other[2], output_weight, swapped)
    home2 = [send(part, turn) for part, turn in zip(last, (to_y(2),) + turns)]
    held = fan(after(info, *last), held, got)
    parts = [held[0]] + [send(part, to_h(d + 1)) for d, part in enumerate(held[1:])]
    near1, home1 = second_half(1, got1, *held, *home0)
    parts[0] = after(parts[0], *near1)
    down, up = settle(parts)
    order = (0, 2, 1)
    t = lowrank(down, send(down, swap_z), [own[i] for i in order], [other[i] for i in order])
    t = after(t + send(t, pair_y(1)), *home1, *home2)
    t = t + send(t, pair_y(2))

    result = None
    for chunk, mine, theirs, gots in zip(chunks, own, other, (home0, home1, home2)):
        result = home(
            info, chunk, mine, theirs, output_weight, swapped, gots, t, up, residual, gate, request_count, result
        )
    return result


def solution(mesh):
    placed = (
        P("rep", None, "tp"),
        P("rep", None, "tp"),
        P("rep", None, "tp"),
        P("tp", None),
        P("rep", "tp", None),
        P("rep", None, "tp"),
        P("rep", None, "tp"),
        P("rep", "tp"),
        P(),
        P(),
        P(),
    )
    return jax.shard_map(
        per_device, mesh=mesh, in_specs=placed, out_specs=P("rep", None, "tp"), check_vma=False
    )
```
